32 devices in a mesh: dp: 4 (over x, core), ctx: 4 (over z), tensor: 2 (over y).
Axes of the slice: x: 2, y: 2, z: 4, core: 2. Of those that a mesh axis runs over, the one named last changes fastest.
Arguments:
- inputs: bfloat16 [4, 2048, 1024], P('dp', 'ctx'), may hold values from -6 to 6
- qkv_weight: bfloat16 [1024, 3, 1024], P('dp', None, 'tensor'), may hold values from -0.1875 to 0.1875
- qv_bias: bfloat16 [2, 16, 64], P(None, 'tensor', 'dp'), may hold values from -3 to 3
- out_weight: bfloat16 [1024, 1024], P('tensor', 'dp'), may hold values from -1.5 to 1.5
- out_bias: bfloat16 [1024], P('dp'), may hold values from -2 to 2
- up_weight: bfloat16 [1024, 4096], P('dp', 'tensor'), may hold values from -0.1875 to 0.1875
- up_bias: bfloat16 [64, 64], P('tensor', 'dp'), may hold values from -3 to 3
- down_weight: bfloat16 [4096, 1024], P('tensor', 'dp'), may hold values from -0.09375 to 0.09375
- down_bias: bfloat16 [1024], P('dp'), may hold values from -2 to 2
- first_gain: bfloat16 [1024], P('dp'), may hold values from 0.099609375 to 1.8984375
- first_shift: bfloat16 [1024], P('dp'), may hold values from -2 to 2
- second_gain: bfloat16 [1024], P('dp'), may hold values from 0.099609375 to 1.8984375
- second_shift: bfloat16 [1024], P('dp'), may hold values from -2 to 2
- grad_output: bfloat16 [4, 2048, 1024], P('dp', 'ctx'), may hold values from -6 to 6
Outputs:
- output: bfloat16 [4, 2048, 1024], P('dp', 'ctx')
- grad_inputs: bfloat16 [4, 2048, 1024], P('dp', 'ctx')
- grad_qkv_weight: float32 [1024, 3, 1024], P('dp', None, 'tensor')
- grad_qv_bias: float32 [2, 16, 64], P(None, 'tensor', 'dp')
- grad_out_weight: float32 [1024, 1024], P('tensor', 'dp')
- grad_out_bias: float32 [1024], P('dp')
- grad_up_weight: float32 [1024, 4096], P('dp', 'tensor')
- grad_up_bias: float32 [64, 64], P('tensor', 'dp')
- grad_down_weight: float32 [4096, 1024], P('tensor', 'dp')
- grad_down_bias: float32 [1024], P('dp')
- grad_first_gain: float32 [1024], P('dp')
- grad_first_shift: float32 [1024], P('dp')
- grad_second_gain: float32 [1024], P('dp')
- grad_second_shift: float32 [1024], P('dp')
The draws below stay inside these ranges and needn't reach their ends.
All inputs are finite; a program needn't handle non-finite values.
Results may differ from the reference program's by a relative error of at most 0.023.
Values may be sent and summed in bfloat16 or wider, within the bound.
A program may use at most 320 MiB of HBM per device.

```python
import jax
import jax.numpy as jnp
from jax import lax

D = 1024
HEADS = 16
HEAD_DIM = 64
FF = 4096
BLOCK = 512
SEQS = 4
LENGTH = 2048
N_CTX = 4


def levels(key, dims, split, smallest, top_value):
    def one(position, shards_of):
        draws = jax.random.uniform(jax.random.fold_in(jax.random.fold_in(key, 6), position), (shards_of,), jnp.float32, smallest / len(split), top_value / len(split))
        return jnp.repeat(jnp.exp(draws), dims[position] // shards_of).reshape((-1,) + (1,) * (len(dims) - position - 1))

    level = one(*split[0])
    for cut in split[1:]:
        level = level * one(*cut)
    return level


def bell_draw(stream_key, extent, scale, most, pieces=(), held_as=jnp.bfloat16):
    drawn = jax.random.normal(stream_key, extent, jnp.float32) * scale
    if len(pieces) > 0:
        drawn = levels(stream_key, extent, pieces, -0.22, 0.18) * drawn
    return jnp.clip(drawn, min=-most, max=most).astype(held_as)


def setup_inputs(seed: int = 0) -> dict:
    streams_of = jax.random.split(jax.random.key(seed), 15)
    inputs = bell_draw(streams_of[0], (SEQS, LENGTH, D), 1.0, 6.0, ((0, 4), (1, 4)))
    qkv_weight = bell_draw(streams_of[1], (D, 3, D), D ** -0.5, 0.1875, ((0, 4), (2, 2)))
    qv_bias = bell_draw(streams_of[2], (2, HEADS, HEAD_DIM), 0.5, 3.0, ((1, 2), (2, 4)))
    out_weight = bell_draw(streams_of[3], (D, D), (D // 64) ** -0.5, 1.5, ((0, 2), (1, 4)))
    out_bias = bell_draw(streams_of[4], (D,), 0.3, 2.0, ((0, 4),))
    up_weight = bell_draw(streams_of[5], (D, FF), D ** -0.5, 0.1875, ((0, 4), (1, 2)))
    up_bias = bell_draw(streams_of[6], (FF // 64, 64), 0.5, 3.0, ((0, 2), (1, 4)))
    down_weight = bell_draw(streams_of[7], (FF, D), FF ** -0.5, 0.09375, ((0, 2), (1, 4)))
    down_bias = bell_draw(streams_of[8], (D,), 0.3, 2.0, ((0, 4),))
    first_gain = jnp.clip(1.0 + 0.18 * jax.random.normal(streams_of[9], (D,), jnp.float32), 0.099609375, 1.8984375).astype(jnp.bfloat16)
    first_shift = bell_draw(streams_of[10], (D,), 0.3, 2.0, ((0, 4),))
    second_gain = jnp.clip(1.0 + 0.18 * jax.random.normal(streams_of[11], (D,), jnp.float32), 0.099609375, 1.8984375).astype(jnp.bfloat16)
    second_shift = bell_draw(streams_of[12], (D,), 0.3, 2.0, ((0, 4),))
    grad_output = bell_draw(streams_of[13], (SEQS, LENGTH, D), 1.0, 6.0, ((0, 4), (1, 4)))
    return dict(inputs=inputs, qkv_weight=qkv_weight, qv_bias=qv_bias, out_weight=out_weight, out_bias=out_bias, up_weight=up_weight, up_bias=up_bias, down_weight=down_weight, down_bias=down_bias, first_gain=first_gain, first_shift=first_shift, second_gain=second_gain, second_shift=second_shift, grad_output=grad_output)


@jax.custom_vjp
def low(v):
    return lax.optimization_barrier(v.astype(jnp.bfloat16)).astype(jnp.float32)

@jax.custom_vjp
def low_back(v):
    return v

def low_keep(v):
    return (low(v), None)

def low_pass(kept, grad):
    return (grad,)

def back_keep(v):
    return (v, None)

def back_low(kept, grad):
    return (low(grad),)
low.defvjp(low_keep, low_pass)
low_back.defvjp(back_keep, back_low)

def layer_norm(values, gain, shift):
    center = values - lax.optimization_barrier(jnp.mean(values, axis=-1, keepdims=True))
    spread = lax.optimization_barrier(jnp.mean(center * center, axis=-1, keepdims=True))
    return center * lax.rsqrt(spread + 1e-05) * gain + shift

def attend(query, keys, values):
    q_heads = query.reshape(N_CTX, BLOCK, HEADS, HEAD_DIM)
    k_heads = keys.reshape(LENGTH, HEADS, HEAD_DIM)
    v_heads = values.reshape(LENGTH, HEADS, HEAD_DIM)
    key_pos = jnp.arange(LENGTH)

    @jax.checkpoint
    def one_block(item):
        q_block, start = item
        scores = low_back(jnp.einsum('qhd,khd->hqk', q_block, k_heads, precision=lax.Precision.HIGHEST) * 0.125)
        q_pos = start + jnp.arange(BLOCK)
        allowed = key_pos[None, :] <= q_pos[:, None]
        scores = jnp.where(allowed[None], scores, -1e+30)
        probs = low(jax.nn.softmax(scores, axis=-1))
        return jnp.einsum('hqk,khd->qhd', probs, v_heads, precision=lax.Precision.HIGHEST)
    result = lax.map(one_block, (q_heads, jnp.arange(N_CTX) * BLOCK))
    return result.reshape(LENGTH, D)

def forward(rows, params):
    qkv_w, qv_b, out_w, out_b, up_w, up_b, down_w, down_b, gain_one, shift_one, gain_two, shift_two = params
    high = lax.Precision.HIGHEST
    normed_one = low(layer_norm(rows, gain_one, shift_one))
    mixed = jnp.einsum('td,dch->tch', normed_one, qkv_w, precision=high)
    query = low(low_back(mixed[:, 0] + qv_b[0].reshape(-1)))
    keys = low(low_back(mixed[:, 1]))
    values = low(low_back(mixed[:, 2] + qv_b[1].reshape(-1)))
    attended = low(low_back(attend(query, keys, values)))
    branch = low_back(jnp.dot(attended, out_w, precision=high) + out_b)
    resid = rows + branch
    normed_two = low(layer_norm(resid, gain_two, shift_two))
    hidden_pre = low_back(jnp.dot(normed_two, up_w, precision=high) + up_b.reshape(-1))
    hidden_act = low(jax.nn.gelu(hidden_pre, approximate=True))
    return resid + jnp.dot(hidden_act, down_w, precision=high) + down_b

def reference(inputs, qkv_weight, qv_bias, out_weight, out_bias, up_weight, up_bias, down_weight, down_bias, first_gain, first_shift, second_gain, second_shift, grad_output):
    params = tuple((item.astype(jnp.float32) for item in (qkv_weight, qv_bias, out_weight, out_bias, up_weight, up_bias, down_weight, down_bias, first_gain, first_shift, second_gain, second_shift)))

    def per_sequence(totals, item):
        rows, cotangent = item
        result, pull = jax.vjp(forward, rows.astype(jnp.float32), params)
        grad_rows, grad_params = pull(cotangent.astype(jnp.float32))
        totals = jax.tree.map(jnp.add, totals, grad_params)
        return (totals, (result.astype(jnp.bfloat16), grad_rows.astype(jnp.bfloat16)))
    zeros = jax.tree.map(jnp.zeros_like, params)
    grads, (output, grad_inputs) = lax.scan(per_sequence, zeros, (inputs, grad_output))
    return (output, grad_inputs, grads[0], grads[1], grads[2], grads[3], grads[4], grads[5], grads[6], grads[7], grads[8], grads[9], grads[10], grads[11])
```

```python
import jax
import jax.numpy as jnp
from jax import lax
from jax.experimental import pallas as pl
from jax.experimental.pallas import tpu as pltpu
from jax.sharding import PartitionSpec as P

HEAD_DIM = 64
F32 = jnp.float32
BF16 = jnp.bfloat16
ROWS_BY_ROWS = (((0,), (0,)), ((), ()))
LAST_BY_LAST = (((1,), (1,)), ((), ()))


def ahead(value, axis, steps):
    count = lax.axis_size(axis)
    first, last = (max(0, -steps), min(count, count - steps))
    return lax.ppermute(value, axis, [(source, source + steps) for source in range(first, last)])


def pair_sum(value):
    low = value.astype(BF16)
    if lax.axis_size("tensor") == 2:
        other = lax.ppermute(low, "tensor", [(0, 1), (1, 0)])
        return low.astype(F32) + other.astype(F32)
    return lax.psum(low, "tensor").astype(F32)


def norm_parts(values):
    center = values - jnp.mean(values, axis=-1, keepdims=True)
    scale = lax.rsqrt(jnp.mean(center * center, axis=-1, keepdims=True) + 1e-05)
    return center * scale, scale


def norm_back(grad, xhat, scale, gain):
    scaled = grad * gain
    return scale * (
        scaled
        - jnp.mean(scaled, axis=-1, keepdims=True)
        - xhat * jnp.mean(scaled * xhat, axis=-1, keepdims=True)
    )


def causal(scores):
    key_pos = lax.broadcasted_iota(jnp.int32, scores.shape, 0)
    query_pos = lax.broadcasted_iota(jnp.int32, scores.shape, 1)
    return jnp.where(key_pos <= query_pos, scores, -1e30)


def scores_of(q_ref, k_ref):
    scaled = q_ref[...] * jnp.asarray(0.125, BF16)
    return lax.dot_general(k_ref[...], scaled, ROWS_BY_ROWS, preferred_element_type=F32)


def first_tile(q_ref, k_ref, v_ref, peak_ref, total_ref, accum_ref):
    scores = causal(scores_of(q_ref, k_ref))
    peak = jnp.max(scores, axis=0, keepdims=True)
    weights = jnp.exp(scores - peak)
    peak_ref[0] = peak
    total_ref[0] = jnp.sum(weights, axis=0, keepdims=True)
    accum_ref[...] = jnp.dot(v_ref[...], weights.astype(BF16), preferred_element_type=F32)


def next_tile(distance, place_ref, q_ref, k_ref, v_ref, p_ref, t_ref, a_ref, peak_ref, total_ref, accum_ref):
    valid = place_ref[0] >= distance

    @pl.when(valid)
    def run():
        scores = scores_of(q_ref, k_ref)
        old = p_ref[0]
        peak = jnp.maximum(old, jnp.max(scores, axis=0, keepdims=True))
        weights = jnp.exp(scores - peak)
        fade = jnp.exp(old - peak)
        peak_ref[0] = peak
        total_ref[0] = t_ref[0] * fade + jnp.sum(weights, axis=0, keepdims=True)
        accum_ref[...] = a_ref[...] * fade + jnp.dot(
            v_ref[...], weights.astype(BF16), preferred_element_type=F32
        )

    @pl.when(jnp.logical_not(valid))
    def keep():
        peak_ref[...] = p_ref[...]
        total_ref[...] = t_ref[...]
        accum_ref[...] = a_ref[...]


def back_tile(distance, place_ref, q_ref, k_ref, v_ref, g_ref, lse_ref, delta_ref, dq_ref, dk_ref, dv_ref):
    valid = place_ref[0] >= distance

    @pl.when(valid)
    def run():
        scores = scores_of(q_ref, k_ref)
        if distance == 0:
            scores = causal(scores)
        probs = jnp.exp(scores - lse_ref[0])
        grad_probs = lax.dot_general(
            v_ref[...], g_ref[...], ROWS_BY_ROWS, preferred_element_type=F32
        )
        grad_scores = (probs * (grad_probs - delta_ref[0])).astype(BF16)
        dv_ref[...] = lax.dot_general(
            g_ref[...], probs.astype(BF16), LAST_BY_LAST, preferred_element_type=F32
        )
        dk_ref[...] = 0.125 * lax.dot_general(
            q_ref[...], grad_scores, LAST_BY_LAST, preferred_element_type=F32
        )
        dq_ref[...] = 0.125 * jnp.dot(k_ref[...], grad_scores, preferred_element_type=F32)

    @pl.when(jnp.logical_not(valid))
    def clear():
        dq_ref[...] = jnp.zeros_like(dq_ref)
        dk_ref[...] = jnp.zeros_like(dk_ref)
        dv_ref[...] = jnp.zeros_like(dv_ref)


def tile_call(kernel, place, wide, stats, flops, order):
    width, count = wide[0].shape
    heads = width // HEAD_DIM
    wide_spec = pl.BlockSpec((HEAD_DIM, count), lambda h: (h, 0))
    stat_spec = pl.BlockSpec((1, 1, count), lambda h: (h, 0, 0))
    specs = {"w": wide_spec, "s": stat_spec}
    scalars = [] if place is None else [place]
    scalar_specs = [] if place is None else [pl.BlockSpec(memory_space=pltpu.SMEM)]
    wide_shape = jax.ShapeDtypeStruct((width, count), F32)
    stat_shape = jax.ShapeDtypeStruct((heads, 1, count), F32)
    ins, outs = order
    wide, stats = (list(wide), list(stats))
    args = [wide.pop(0) if kind == "w" else stats.pop(0) for kind in ins]
    return pl.pallas_call(
        kernel,
        grid=(heads,),
        in_specs=scalar_specs + [specs[kind] for kind in ins],
        out_specs=[specs[kind] for kind in outs],
        out_shape=[wide_shape if kind == "w" else stat_shape for kind in outs],
        compiler_params=pltpu.CompilerParams(vmem_limit_bytes=32 * 1024 * 1024),
        cost_estimate=pl.CostEstimate(
            flops=flops * 2 * width * count * count,
            bytes_accessed=6 * width * count * 4,
            transcendentals=heads * count * count,
        ),
    )(*scalars, *args)


def local(
    inputs,
    qkv_weight,
    qv_bias,
    out_weight,
    out_bias,
    up_weight,
    up_bias,
    down_weight,
    down_bias,
    first_gain,
    first_shift,
    second_gain,
    second_shift,
    grad_output,
):
    shape = inputs.shape
    width = shape[-1]
    rows = inputs.reshape(-1, width).astype(F32)
    count = rows.shape[0]
    ctx_size = lax.axis_size("ctx")
    dp_size = lax.axis_size("dp")
    dp_place = lax.axis_index("dp")
    place = lax.axis_index("ctx").astype(jnp.int32).reshape(1)

    attn_in = lax.all_gather(jnp.swapaxes(qkv_weight, 0, 1), "dp", axis=1, tiled=True)
    small = (
        first_gain,
        first_shift,
        second_gain,
        second_shift,
        out_bias,
        down_bias,
        qv_bias,
        up_bias,
    )
    packed = lax.all_gather(jnp.concatenate([item.reshape(-1) for item in small]), "dp")
    packed = packed.astype(F32)
    parts = []
    start = 0
    for item in small:
        part = packed[:, start : start + item.size].reshape((dp_size,) + item.shape)
        start += item.size
        parts.append(jnp.moveaxis(part, 0, -2).reshape(item.shape[:-1] + (-1,)))
    gain_one, shift_one, gain_two, shift_two, bias_out, bias_down, bias_in, bias_up = parts
    attn_out = lax.all_gather(out_weight, "dp", axis=1, tiled=True)
    mlp_up = lax.all_gather(up_weight, "dp", axis=0, tiled=True)
    mlp_down = lax.all_gather(down_weight, "dp", axis=1, tiled=True)

    half_width = attn_in.shape[2]
    heads = half_width // HEAD_DIM
    xhat_one, scale_one = norm_parts(rows)
    normed_low = (xhat_one * gain_one + shift_one).astype(BF16)
    bias_in = bias_in.reshape(2, half_width, 1)
    mixed = jnp.einsum("td,cdh->cht", normed_low, attn_in, preferred_element_type=F32)
    query = (mixed[0] + bias_in[0]).astype(BF16)
    keys = mixed[1].astype(BF16)
    values = (mixed[2] + bias_in[1]).astype(BF16)

    blocks = [jnp.concatenate([keys, values], axis=0)]
    for distance in range(1, ctx_size):
        blocks.append(ahead(blocks[-1], "ctx", 1))
    peak, total, accum = tile_call(
        first_tile, None, (query, keys, values), (), 2, ("www", "ssw")
    )
    pairs = [(keys, values)]
    for distance in range(1, ctx_size):
        block = blocks[distance]
        pairs.append((block[:half_width], block[half_width:]))

        def step(*refs, distance=distance):
            next_tile(distance, *refs)

        peak, total, accum = tile_call(
            step,
            place,
            (query, *pairs[distance], accum),
            (peak, total),
            2,
            ("wwwssw", "ssw"),
        )
    attn_heads = accum.reshape(heads, HEAD_DIM, count) / total
    log_total = peak + jnp.log(total)
    attended_low = attn_heads.reshape(half_width, count).astype(BF16)

    branch = pair_sum(jnp.einsum("ht,hd->td", attended_low, attn_out, preferred_element_type=F32))
    resid = rows + branch + bias_out
    xhat_two, scale_two = norm_parts(resid)
    normed_two_low = (xhat_two * gain_two + shift_two).astype(BF16)
    hidden_pre = jnp.dot(normed_two_low, mlp_up, preferred_element_type=F32) + bias_up.reshape(-1)
    hidden_act, gelu_pull = jax.vjp(lambda pre: jax.nn.gelu(pre, approximate=True), hidden_pre)
    hidden_act = hidden_act.astype(BF16)

    grad_rows = grad_output.reshape(count, width)
    grad_float = grad_rows.astype(F32)
    grad_bias_down = jnp.sum(grad_float, axis=0)
    grad_act = jnp.einsum("td,fd->tf", grad_rows, mlp_down, preferred_element_type=F32)
    grad_pre = gelu_pull(grad_act)[0].astype(BF16)
    grad_normed_two = pair_sum(
        jnp.einsum("tf,df->td", grad_pre, mlp_up, preferred_element_type=F32)
    )
    mlp_part = pair_sum(jnp.dot(hidden_act, mlp_down, preferred_element_type=F32))
    output = (resid + mlp_part + bias_down).astype(BF16).reshape(shape)

    def scattered(value, dimension):
        return lax.psum_scatter(
            value.astype(BF16), "dp", scatter_dimension=dimension, tiled=True
        )

    grad_down = scattered(
        jnp.einsum("tf,td->fd", hidden_act, grad_rows, preferred_element_type=F32), 1
    )
    grad_bias_up = jnp.sum(grad_pre, axis=0, dtype=F32)
    grad_up = scattered(
        jnp.einsum("td,tf->df", normed_two_low, grad_pre, preferred_element_type=F32), 0
    )

    grad_gain_two = jnp.sum(grad_normed_two * xhat_two, axis=0)
    grad_shift_two = jnp.sum(grad_normed_two, axis=0)
    grad_resid = grad_float + norm_back(grad_normed_two, xhat_two, scale_two, gain_two)
    grad_branch = grad_resid.astype(BF16)
    grad_bias_out = jnp.sum(grad_branch, axis=0, dtype=F32)
    grad_attended = jnp.einsum(
        "td,hd->ht", grad_branch, attn_out, preferred_element_type=F32
    ).astype(BF16)
    grad_heads = grad_attended.astype(F32).reshape(heads, HEAD_DIM, count)
    delta = jnp.sum(grad_heads * attn_heads, axis=1, keepdims=True)
    grad_out = scattered(
        jnp.einsum("ht,td->hd", attended_low, grad_branch, preferred_element_type=F32), 1
    )

    grad_query = 0.0
    arrived = None
    for distance in range(ctx_size - 1, -1, -1):

        def back_step(*refs, distance=distance):
            back_tile(distance, *refs)

        part_query, part_keys, part_values = tile_call(
            back_step,
            place,
            (query, *pairs[distance], grad_attended),
            (log_total, delta),
            5,
            ("wwwwss", "www"),
        )
        grad_query = grad_query + part_query
        block = jnp.concatenate([part_keys, part_values], axis=0)
        if arrived is not None:
            block = block + arrived.astype(F32)
        block = block.astype(BF16)
        if distance > 0:
            arrived = ahead(block, "ctx", -1)
    grad_mixed = jnp.concatenate([grad_query.astype(BF16), block], axis=0)
    grad_mixed = grad_mixed.reshape(3, half_width, count)
    grad_bias_in = jnp.sum(grad_mixed[0::2], axis=2, dtype=F32)
    grad_normed_one = pair_sum(
        jnp.einsum("cht,cdh->td", grad_mixed, attn_in, preferred_element_type=F32)
    )
    grad_attn_in = scattered(
        jnp.einsum("td,cht->cdh", normed_low, grad_mixed, preferred_element_type=F32), 1
    )
    grad_gain_one = jnp.sum(grad_normed_one * xhat_one, axis=0)
    grad_shift_one = jnp.sum(grad_normed_one, axis=0)
    grad_inputs = grad_resid + norm_back(grad_normed_one, xhat_one, scale_one, gain_one)
    grad_inputs = grad_inputs.astype(BF16).reshape(shape)

    grad_up, grad_down = [lax.psum(item, "ctx").astype(F32) for item in (grad_up, grad_down)]
    grad_out, grad_attn_in = [
        lax.psum(item, "ctx").astype(F32) for item in (grad_out, grad_attn_in)
    ]
    grad_attn_in = jnp.swapaxes(grad_attn_in, 0, 1)

    grads_small = (
        grad_gain_one,
        grad_shift_one,
        grad_gain_two,
        grad_shift_two,
        grad_bias_out,
        grad_bias_down,
        grad_bias_in,
        grad_bias_up,
    )
    summed = lax.psum(jnp.concatenate([item.reshape(-1) for item in grads_small]), ("dp", "ctx"))
    small_out = []
    start = 0
    for item in small:
        whole = summed[start : start + item.size * dp_size]
        start += item.size * dp_size
        whole = whole.reshape(item.shape[:-1] + (dp_size, item.shape[-1]))
        small_out.append(lax.dynamic_index_in_dim(whole, dp_place, whole.ndim - 2, False))
    (
        grad_gain_one,
        grad_shift_one,
        grad_gain_two,
        grad_shift_two,
        grad_bias_out,
        grad_bias_down,
        grad_bias_in,
        grad_bias_up,
    ) = small_out
    return (
        output,
        grad_inputs,
        grad_attn_in,
        grad_bias_in,
        grad_out,
        grad_bias_out,
        grad_up,
        grad_bias_up,
        grad_down,
        grad_bias_down,
        grad_gain_one,
        grad_shift_one,
        grad_gain_two,
        grad_shift_two,
    )


def solution(mesh):
    in_specs = (
        P("dp", "ctx", None),
        P("dp", None, "tensor"),
        P(None, "tensor", "dp"),
        P("tensor", "dp"),
        P("dp"),
        P("dp", "tensor"),
        P("tensor", "dp"),
        P("tensor", "dp"),
        P("dp"),
        P("dp"),
        P("dp"),
        P("dp"),
        P("dp"),
        P("dp", "ctx", None),
    )
    out_specs = (
        P("dp", "ctx", None),
        P("dp", "ctx", None),
        P("dp", None, "tensor"),
        P(None, "tensor", "dp"),
        P("tensor", "dp"),
        P("dp"),
        P("dp", "tensor"),
        P("tensor", "dp"),
        P("tensor", "dp"),
        P("dp"),
        P("dp"),
        P("dp"),
        P("dp"),
        P("dp"),
    )
    return jax.shard_map(local, mesh=mesh, in_specs=in_specs, out_specs=out_specs, check_vma=False)
```

```python
import jax
import jax.numpy as jnp
from jax import lax
from jax.experimental import pallas as pl
from jax.experimental.pallas import tpu as pltpu
from jax.sharding import PartitionSpec as P

HEAD_DIM = 64
F32 = jnp.float32
BF16 = jnp.bfloat16
ROWS_BY_ROWS = (((0,), (0,)), ((), ()))
LAST_BY_LAST = (((1,), (1,)), ((), ()))


def ahead(value, axis, steps):
    count = lax.axis_size(axis)
    first, last = (max(0, -steps), min(count, count - steps))
    return lax.ppermute(value, axis, [(source, source + steps) for source in range(first, last)])


def pair_sum(value):
    low = value.astype(BF16)
    if lax.axis_size("tensor") == 2:
        other = lax.ppermute(low, "tensor", [(0, 1), (1, 0)])
        return low.astype(F32) + other.astype(F32)
    return lax.psum(low, "tensor").astype(F32)


def flipped(value, axis, bit):
    count = lax.axis_size(axis)
    return lax.ppermute(value, axis, [(source, source ^ bit) for source in range(count)])


def gather_shards(shard):
    mine = lax.axis_index("dp")
    beside = flipped(shard, "dp", 1)
    across = flipped(shard, "dp", 2)
    corner = flipped(across, "dp", 1)
    whole = jnp.zeros((4,) + shard.shape, shard.dtype)
    for bit, item in enumerate((shard, beside, across, corner)):
        whole = lax.dynamic_update_index_in_dim(whole, item, mine ^ bit, 0)
    return whole


def shard_columns(rows, core, high):
    size = rows.shape[1] // 4
    return lax.dynamic_slice_in_dim(rows, (2 * high + core) * size, size, 1)


def scatter_product(rows, product):
    mine = lax.axis_index("dp")
    core, high = mine % 2, mine // 2
    sent = [product(shard_columns(rows, 1 - core, bit)).astype(BF16) for bit in (1 - high, high)]
    sent = [flipped(item, "dp", 1) for item in sent]
    kept = [product(shard_columns(rows, core, bit)) for bit in (1 - high, high)]
    away, home = [own + other.astype(F32) for own, other in zip(kept, sent)]
    return home + flipped(away.astype(BF16), "dp", 2).astype(F32)


def ctx_total(value):
    count = lax.axis_size("ctx")
    mine = lax.axis_index("ctx")
    chunks = value.astype(BF16).reshape((count, -1) + value.shape[1:])
    total = lax.dynamic_index_in_dim(chunks, mine, 0, False).astype(F32)
    for step in range(1, count):
        chunk = lax.dynamic_index_in_dim(chunks, (mine + step) % count, 0, False)
        pairs = [(source, (source + step) % count) for source in range(count)]
        total = total + lax.ppermute(chunk, "ctx", pairs).astype(F32)
    total = total.astype(BF16)
    whole = lax.dynamic_update_index_in_dim(jnp.zeros_like(chunks), total, mine, 0)
    for step in range(1, count):
        pairs = [(source, (source + step) % count) for source in range(count)]
        other = lax.ppermute(total, "ctx", pairs)
        whole = lax.dynamic_update_index_in_dim(whole, other, (mine + count - step) % count, 0)
    return whole.reshape(value.shape).astype(F32)


def small_total(value):
    for axis in ("dp", "ctx"):
        bit = 1
        while bit < lax.axis_size(axis):
            value = value + flipped(value, axis, bit)
            bit *= 2
    return value


def norm_parts(values):
    center = values - jnp.mean(values, axis=-1, keepdims=True)
    scale = lax.rsqrt(jnp.mean(center * center, axis=-1, keepdims=True) + 1e-05)
    return center * scale, scale


def norm_back(grad, xhat, scale, gain):
    scaled = grad * gain
    return scale * (
        scaled
        - jnp.mean(scaled, axis=-1, keepdims=True)
        - xhat * jnp.mean(scaled * xhat, axis=-1, keepdims=True)
    )


def causal(scores):
    key_pos = lax.broadcasted_iota(jnp.int32, scores.shape, 0)
    query_pos = lax.broadcasted_iota(jnp.int32, scores.shape, 1)
    return jnp.where(key_pos <= query_pos, scores, -1e30)


def scores_of(q_ref, k_ref):
    scaled = q_ref[...] * jnp.asarray(0.125, BF16)
    return lax.dot_general(k_ref[...], scaled, ROWS_BY_ROWS, preferred_element_type=F32)


def first_tile(q_ref, k_ref, v_ref, peak_ref, total_ref, accum_ref):
    scores = causal(scores_of(q_ref, k_ref))
    peak = jnp.max(scores, axis=0, keepdims=True)
    weights = jnp.exp(scores - peak)
    peak_ref[0] = peak
    total_ref[0] = jnp.sum(weights, axis=0, keepdims=True)
    accum_ref[...] = jnp.dot(v_ref[...], weights.astype(BF16), preferred_element_type=F32)


def next_tile(distance, place_ref, q_ref, k_ref, v_ref, p_ref, t_ref, a_ref, peak_ref, total_ref, accum_ref):
    valid = place_ref[0] >= distance

    @pl.when(valid)
    def run():
        scores = scores_of(q_ref, k_ref)
        old = p_ref[0]
        peak = jnp.maximum(old, jnp.max(scores, axis=0, keepdims=True))
        weights = jnp.exp(scores - peak)
        fade = jnp.exp(old - peak)
        peak_ref[0] = peak
        total_ref[0] = t_ref[0] * fade + jnp.sum(weights, axis=0, keepdims=True)
        accum_ref[...] = a_ref[...] * fade + jnp.dot(
            v_ref[...], weights.astype(BF16), preferred_element_type=F32
        )

    @pl.when(jnp.logical_not(valid))
    def keep():
        peak_ref[...] = p_ref[...]
        total_ref[...] = t_ref[...]
        accum_ref[...] = a_ref[...]


def back_tile(distance, place_ref, q_ref, k_ref, v_ref, g_ref, lse_ref, delta_ref, dq_ref, dk_ref, dv_ref):
    valid = place_ref[0] >= distance

    @pl.when(valid)
    def run():
        scores = scores_of(q_ref, k_ref)
        if distance == 0:
            scores = causal(scores)
        probs = jnp.exp(scores - lse_ref[0])
        grad_probs = lax.dot_general(
            v_ref[...], g_ref[...], ROWS_BY_ROWS, preferred_element_type=F32
        )
        grad_scores = (probs * (grad_probs - delta_ref[0])).astype(BF16)
        dv_ref[...] = lax.dot_general(
            g_ref[...], probs.astype(BF16), LAST_BY_LAST, preferred_element_type=F32
        )
        dk_ref[...] = 0.125 * lax.dot_general(
            q_ref[...], grad_scores, LAST_BY_LAST, preferred_element_type=F32
        )
        dq_ref[...] = 0.125 * jnp.dot(k_ref[...], grad_scores, preferred_element_type=F32)

    @pl.when(jnp.logical_not(valid))
    def clear():
        dq_ref[...] = jnp.zeros_like(dq_ref)
        dk_ref[...] = jnp.zeros_like(dk_ref)
        dv_ref[...] = jnp.zeros_like(dv_ref)


def tile_call(kernel, place, wide, stats, flops, order):
    width, count = wide[0].shape
    heads = width // HEAD_DIM
    wide_spec = pl.BlockSpec((HEAD_DIM, count), lambda h: (h, 0))
    stat_spec = pl.BlockSpec((1, 1, count), lambda h: (h, 0, 0))
    specs = {"w": wide_spec, "s": stat_spec}
    scalars = [] if place is None else [place]
    scalar_specs = [] if place is None else [pl.BlockSpec(memory_space=pltpu.SMEM)]
    wide_shape = jax.ShapeDtypeStruct((width, count), F32)
    stat_shape = jax.ShapeDtypeStruct((heads, 1, count), F32)
    ins, outs = order
    wide, stats = (list(wide), list(stats))
    args = [wide.pop(0) if kind == "w" else stats.pop(0) for kind in ins]
    return pl.pallas_call(
        kernel,
        grid=(heads,),
        in_specs=scalar_specs + [specs[kind] for kind in ins],
        out_specs=[specs[kind] for kind in outs],
        out_shape=[wide_shape if kind == "w" else stat_shape for kind in outs],
        compiler_params=pltpu.CompilerParams(vmem_limit_bytes=32 * 1024 * 1024),
        cost_estimate=pl.CostEstimate(
            flops=flops * 2 * width * count * count,
            bytes_accessed=6 * width * count * 4,
            transcendentals=heads * count * count,
        ),
    )(*scalars, *args)


def local(
    inputs,
    qkv_weight,
    qv_bias,
    out_weight,
    out_bias,
    up_weight,
    up_bias,
    down_weight,
    down_bias,
    first_gain,
    first_shift,
    second_gain,
    second_shift,
    grad_output,
):
    shape = inputs.shape
    width = shape[-1]
    rows = inputs.reshape(-1, width).astype(F32)
    count = rows.shape[0]
    ctx_size = lax.axis_size("ctx")
    dp_size = lax.axis_size("dp")
    dp_place = lax.axis_index("dp")
    place = lax.axis_index("ctx").astype(jnp.int32).reshape(1)

    kv_in = gather_shards(jnp.swapaxes(qkv_weight[:, 1:], 0, 1))
    kv_in = jnp.swapaxes(kv_in, 0, 1).reshape(2, width, -1)
    q_in = lax.all_gather(qkv_weight[:, 0], "dp", axis=0, tiled=True)
    small = (
        first_gain,
        first_shift,
        second_gain,
        second_shift,
        out_bias,
        down_bias,
        qv_bias,
        up_bias,
    )
    packed = lax.all_gather(jnp.concatenate([item.reshape(-1) for item in small]), "dp")
    packed = packed.astype(F32)
    parts = []
    start = 0
    for item in small:
        part = packed[:, start : start + item.size].reshape((dp_size,) + item.shape)
        start += item.size
        parts.append(jnp.moveaxis(part, 0, -2).reshape(item.shape[:-1] + (-1,)))
    gain_one, shift_one, gain_two, shift_two, bias_out, bias_down, bias_in, bias_up = parts
    attn_out = lax.all_gather(out_weight, "dp", axis=1, tiled=True)
    mlp_up = lax.all_gather(up_weight, "dp", axis=0, tiled=True)
    mlp_down = lax.all_gather(down_weight, "dp", axis=1, tiled=True)

    half_width = q_in.shape[1]
    heads = half_width // HEAD_DIM
    xhat_one, scale_one = norm_parts(rows)
    normed_low = (xhat_one * gain_one + shift_one).astype(BF16)
    bias_in = bias_in.reshape(2, half_width, 1)
    mixed = jnp.einsum("td,cdh->cht", normed_low, kv_in, preferred_element_type=F32)
    keys = mixed[0].astype(BF16)
    values = (mixed[1] + bias_in[1]).astype(BF16)

    blocks = [jnp.concatenate([keys, values], axis=0)]
    query = jnp.einsum("td,dh->ht", normed_low, q_in, preferred_element_type=F32)
    query = (query + bias_in[0]).astype(BF16)
    for distance in range(1, ctx_size):
        blocks.append(ahead(blocks[-1], "ctx", 1))
    peak, total, accum = tile_call(
        first_tile, None, (query, keys, values), (), 2, ("www", "ssw")
    )
    pairs = [(keys, values)]
    for distance in range(1, ctx_size):
        block = blocks[distance]
        pairs.append((block[:half_width], block[half_width:]))

        def step(*refs, distance=distance):
            next_tile(distance, *refs)

        peak, total, accum = tile_call(
            step,
            place,
            (query, *pairs[distance], accum),
            (peak, total),
            2,
            ("wwwssw", "ssw"),
        )
    attn_heads = accum.reshape(heads, HEAD_DIM, count) / total
    log_total = peak + jnp.log(total)
    attended_low = attn_heads.reshape(half_width, count).astype(BF16)

    branch = pair_sum(jnp.einsum("ht,hd->td", attended_low, attn_out, preferred_element_type=F32))
    resid = rows + branch + bias_out
    xhat_two, scale_two = norm_parts(resid)
    normed_two_low = (xhat_two * gain_two + shift_two).astype(BF16)
    hidden_pre = jnp.dot(normed_two_low, mlp_up, preferred_element_type=F32) + bias_up.reshape(-1)
    hidden_act, gelu_pull = jax.vjp(lambda pre: jax.nn.gelu(pre, approximate=True), hidden_pre)
    hidden_act = hidden_act.astype(BF16)

    grad_rows = grad_output.reshape(count, width)
    grad_float = grad_rows.astype(F32)
    grad_bias_down = jnp.sum(grad_float, axis=0)
    grad_act = jnp.einsum("td,fd->tf", grad_rows, mlp_down, preferred_element_type=F32)
    grad_pre = gelu_pull(grad_act)[0].astype(BF16)
    grad_normed_two = pair_sum(
        jnp.einsum("tf,df->td", grad_pre, mlp_up, preferred_element_type=F32)
    )
    later_act, grad_normed_two = lax.optimization_barrier((hidden_act, grad_normed_two))
    mlp_part = pair_sum(jnp.dot(later_act, mlp_down, preferred_element_type=F32))
    output = (resid + mlp_part + bias_down).astype(BF16).reshape(shape)

    grad_down = scatter_product(
        grad_rows,
        lambda part: jnp.einsum("tf,td->fd", hidden_act, part, preferred_element_type=F32),
    )
    grad_bias_up = jnp.sum(grad_pre, axis=0, dtype=F32)
    grad_up = scatter_product(
        normed_two_low,
        lambda part: jnp.einsum("td,tf->df", part, grad_pre, preferred_element_type=F32),
    )

    grad_gain_two = jnp.sum(grad_normed_two * xhat_two, axis=0)
    grad_shift_two = jnp.sum(grad_normed_two, axis=0)
    grad_resid = grad_float + norm_back(grad_normed_two, xhat_two, scale_two, gain_two)
    grad_branch = grad_resid.astype(BF16)
    grad_bias_out = jnp.sum(grad_branch, axis=0, dtype=F32)
    grad_attended = jnp.einsum(
        "td,hd->ht", grad_branch, attn_out, preferred_element_type=F32
    ).astype(BF16)
    grad_heads = grad_attended.astype(F32).reshape(heads, HEAD_DIM, count)
    delta = jnp.sum(grad_heads * attn_heads, axis=1, keepdims=True)
    grad_out = scatter_product(
        grad_branch,
        lambda part: jnp.einsum("ht,td->hd", attended_low, part, preferred_element_type=F32),
    )

    grad_query = 0.0
    arrived = None
    for distance in range(ctx_size - 1, -1, -1):

        def back_step(*refs, distance=distance):
            back_tile(distance, *refs)

        part_query, part_keys, part_values = tile_call(
            back_step,
            place,
            (query, *pairs[distance], grad_attended),
            (log_total, delta),
            5,
            ("wwwwss", "www"),
        )
        grad_query = grad_query + part_query
        block = jnp.concatenate([part_keys, part_values], axis=0)
        if arrived is not None:
            block = block + arrived.astype(F32)
        block = block.astype(BF16)
        if distance > 0:
            arrived = ahead(block, "ctx", -1)
    grad_mixed = jnp.concatenate([grad_query.astype(BF16), block], axis=0)
    grad_mixed = grad_mixed.reshape(3, half_width, count)
    grad_bias_in = jnp.sum(grad_mixed[0::2], axis=2, dtype=F32)
    grad_normed_one = pair_sum(
        jnp.einsum("ht,dh->td", grad_mixed[0], q_in, preferred_element_type=F32)
        + jnp.einsum("cht,cdh->td", grad_mixed[1:], kv_in, preferred_element_type=F32)
    )
    grad_attn_in = scatter_product(
        normed_low,
        lambda part: jnp.einsum(
            "td,rt->dr", part, grad_mixed.reshape(-1, count), preferred_element_type=F32
        ),
    )
    grad_gain_one = jnp.sum(grad_normed_one * xhat_one, axis=0)
    grad_shift_one = jnp.sum(grad_normed_one, axis=0)
    grad_inputs = grad_resid + norm_back(grad_normed_one, xhat_one, scale_one, gain_one)
    grad_inputs = grad_inputs.astype(BF16).reshape(shape)

    grad_up, grad_down, grad_out = [
        lax.psum(item.astype(BF16), "ctx").astype(F32) for item in (grad_up, grad_down, grad_out)
    ]
    grad_attn_in = ctx_total(grad_attn_in).reshape(-1, 3, half_width)

    grads_small = (
        grad_gain_one,
        grad_shift_one,
        grad_gain_two,
        grad_shift_two,
        grad_bias_out,
        grad_bias_down,
        grad_bias_in,
        grad_bias_up,
    )
    summed = small_total(jnp.concatenate([item.reshape(-1) for item in grads_small]))
    small_out = []
    start = 0
    for item in small:
        whole = summed[start : start + item.size * dp_size]
        start += item.size * dp_size
        whole = whole.reshape(item.shape[:-1] + (dp_size, item.shape[-1]))
        small_out.append(lax.dynamic_index_in_dim(whole, dp_place, whole.ndim - 2, False))
    (
        grad_gain_one,
        grad_shift_one,
        grad_gain_two,
        grad_shift_two,
        grad_bias_out,
        grad_bias_down,
        grad_bias_in,
        grad_bias_up,
    ) = small_out
    return (
        output,
        grad_inputs,
        grad_attn_in,
        grad_bias_in,
        grad_out,
        grad_bias_out,
        grad_up,
        grad_bias_up,
        grad_down,
        grad_bias_down,
        grad_gain_one,
        grad_shift_one,
        grad_gain_two,
        grad_shift_two,
    )


def solution(mesh):
    in_specs = (
        P("dp", "ctx", None),
        P("dp", None, "tensor"),
        P(None, "tensor", "dp"),
        P("tensor", "dp"),
        P("dp"),
        P("dp", "tensor"),
        P("tensor", "dp"),
        P("tensor", "dp"),
        P("dp"),
        P("dp"),
        P("dp"),
        P("dp"),
        P("dp"),
        P("dp", "ctx", None),
    )
    out_specs = (
        P("dp", "ctx", None),
        P("dp", "ctx", None),
        P("dp", None, "tensor"),
        P(None, "tensor", "dp"),
        P("tensor", "dp"),
        P("dp"),
        P("dp", "tensor"),
        P("tensor", "dp"),
        P("tensor", "dp"),
        P("dp"),
        P("dp"),
        P("dp"),
        P("dp"),
        P("dp"),
    )
    return jax.shard_map(local, mesh=mesh, in_specs=in_specs, out_specs=out_specs, check_vma=False)
```

```python
import jax
import jax.numpy as jnp
from jax import lax
from jax.experimental import pallas as pl
from jax.experimental.pallas import tpu as pltpu
from jax.sharding import PartitionSpec as P

HEAD_DIM = 64
F32 = jnp.float32
BF16 = jnp.bfloat16
ROWS_BY_ROWS = (((0,), (0,)), ((), ()))
LAST_BY_LAST = (((1,), (1,)), ((), ()))


def ahead(value, axis, steps):
    count = lax.axis_size(axis)
    first, last = (max(0, -steps), min(count, count - steps))
    return lax.ppermute(value, axis, [(source, source + steps) for source in range(first, last)])


def pair_sum(value):
    low = value.astype(BF16)
    if lax.axis_size("tensor") == 2:
        other = lax.ppermute(low, "tensor", [(0, 1), (1, 0)])
        return low.astype(F32) + other.astype(F32)
    return lax.psum(low, "tensor").astype(F32)


def flipped(value, axis, bit):
    count = lax.axis_size(axis)
    return lax.ppermute(value, axis, [(source, source ^ bit) for source in range(count)])


def gather_shards(shard):
    mine = lax.axis_index("dp")
    beside = flipped(shard, "dp", 1)
    across = flipped(shard, "dp", 2)
    corner = flipped(across, "dp", 1)
    whole = jnp.zeros((4,) + shard.shape, shard.dtype)
    for bit, item in enumerate((shard, beside, across, corner)):
        whole = lax.dynamic_update_index_in_dim(whole, item, mine ^ bit, 0)
    return whole


def shard_columns(rows, core, high):
    size = rows.shape[1] // 4
    return lax.dynamic_slice_in_dim(rows, (2 * high + core) * size, size, 1)


def scatter_product(rows, product):
    mine = lax.axis_index("dp")
    core, high = mine % 2, mine // 2
    sent = [product(shard_columns(rows, 1 - core, bit)).astype(BF16) for bit in (1 - high, high)]
    sent = [flipped(item, "dp", 1) for item in sent]
    kept = [product(shard_columns(rows, core, bit)) for bit in (1 - high, high)]
    away, home = [own + other.astype(F32) for own, other in zip(kept, sent)]
    return home + flipped(away.astype(BF16), "dp", 2).astype(F32)


def ctx_total(value):
    count = lax.axis_size("ctx")
    mine = lax.axis_index("ctx")
    chunks = value.astype(BF16).reshape((count, -1) + value.shape[1:])
    total = lax.dynamic_index_in_dim(chunks, mine, 0, False).astype(F32)
    for step in range(1, count):
        chunk = lax.dynamic_index_in_dim(chunks, (mine + step) % count, 0, False)
        pairs = [(source, (source + step) % count) for source in range(count)]
        total = total + lax.ppermute(chunk, "ctx", pairs).astype(F32)
    total = total.astype(BF16)
    whole = lax.dynamic_update_index_in_dim(jnp.zeros_like(chunks), total, mine, 0)
    for step in range(1, count):
        pairs = [(source, (source + step) % count) for source in range(count)]
        other = lax.ppermute(total, "ctx", pairs)
        whole = lax.dynamic_update_index_in_dim(whole, other, (mine + count - step) % count, 0)
    return whole.reshape(value.shape).astype(F32)


def line_total(value):
    count = lax.axis_size("ctx")
    if count % 2:
        return lax.psum(value.astype(BF16), "ctx").astype(F32)
    mine = lax.axis_index("ctx")
    half = value.shape[0] // 2
    first, second = value[:half], value[half:]
    arrived = 0.0
    hops = [[(hop, hop + 1), (count - 1 - hop, count - 2 - hop)] for hop in range(count - 1)]
    for hop, pairs in enumerate(hops):
        sent = (jnp.where(mine == hop, first, second) + arrived).astype(BF16)
        arrived = lax.ppermute(sent, "ctx", pairs).astype(F32)
    held = (jnp.where(mine == count - 1, first, second) + arrived).astype(BF16)
    total_first, total_second = held, held
    for hop, pairs in enumerate(hops):
        held = lax.ppermute(held, "ctx", pairs)
        total_first = jnp.where(mine == count - 2 - hop, held, total_first)
        total_second = jnp.where(mine == hop + 1, held, total_second)
    return jnp.concatenate([total_first, total_second], axis=0).astype(F32)


def small_total(value):
    for axis in ("dp", "ctx"):
        bit = 1
        while bit < lax.axis_size(axis):
            value = value + flipped(value, axis, bit)
            bit *= 2
    return value


def norm_parts(values):
    center = values - jnp.mean(values, axis=-1, keepdims=True)
    scale = lax.rsqrt(jnp.mean(center * center, axis=-1, keepdims=True) + 1e-05)
    return center * scale, scale


def norm_back(grad, xhat, scale, gain):
    scaled = grad * gain
    return scale * (
        scaled
        - jnp.mean(scaled, axis=-1, keepdims=True)
        - xhat * jnp.mean(scaled * xhat, axis=-1, keepdims=True)
    )


def causal(scores):
    key_pos = lax.broadcasted_iota(jnp.int32, scores.shape, 0)
    query_pos = lax.broadcasted_iota(jnp.int32, scores.shape, 1)
    return jnp.where(key_pos <= query_pos, scores, -1e30)


def scores_of(q_ref, k_ref):
    scaled = q_ref[...] * jnp.asarray(0.125, BF16)
    return lax.dot_general(k_ref[...], scaled, ROWS_BY_ROWS, preferred_element_type=F32)


def first_tile(q_ref, k_ref, v_ref, peak_ref, total_ref, accum_ref):
    scores = causal(scores_of(q_ref, k_ref))
    peak = jnp.max(scores, axis=0, keepdims=True)
    weights = jnp.exp(scores - peak)
    peak_ref[0] = peak
    total_ref[0] = jnp.sum(weights, axis=0, keepdims=True)
    accum_ref[...] = jnp.dot(v_ref[...], weights.astype(BF16), preferred_element_type=F32)


def next_tile(distance, place_ref, q_ref, k_ref, v_ref, p_ref, t_ref, a_ref, peak_ref, total_ref, accum_ref):
    valid = place_ref[0] >= distance

    @pl.when(valid)
    def run():
        scores = scores_of(q_ref, k_ref)
        old = p_ref[0]
        peak = jnp.maximum(old, jnp.max(scores, axis=0, keepdims=True))
        weights = jnp.exp(scores - peak)
        fade = jnp.exp(old - peak)
        peak_ref[0] = peak
        total_ref[0] = t_ref[0] * fade + jnp.sum(weights, axis=0, keepdims=True)
        accum_ref[...] = a_ref[...] * fade + jnp.dot(
            v_ref[...], weights.astype(BF16), preferred_element_type=F32
        )

    @pl.when(jnp.logical_not(valid))
    def keep():
        peak_ref[...] = p_ref[...]
        total_ref[...] = t_ref[...]
        accum_ref[...] = a_ref[...]


def back_tile(distance, place_ref, q_ref, k_ref, v_ref, g_ref, lse_ref, delta_ref, dq_ref, dk_ref, dv_ref):
    valid = place_ref[0] >= distance

    @pl.when(valid)
    def run():
        scores = scores_of(q_ref, k_ref)
        if distance == 0:
            scores = causal(scores)
        probs = jnp.exp(scores - lse_ref[0])
        grad_probs = lax.dot_general(
            v_ref[...], g_ref[...], ROWS_BY_ROWS, preferred_element_type=F32
        )
        grad_scores = (probs * (grad_probs - delta_ref[0])).astype(BF16)
        dv_ref[...] = lax.dot_general(
            g_ref[...], probs.astype(BF16), LAST_BY_LAST, preferred_element_type=F32
        )
        dk_ref[...] = 0.125 * lax.dot_general(
            q_ref[...], grad_scores, LAST_BY_LAST, preferred_element_type=F32
        )
        dq_ref[...] = 0.125 * jnp.dot(k_ref[...], grad_scores, preferred_element_type=F32)

    @pl.when(jnp.logical_not(valid))
    def clear():
        dq_ref[...] = jnp.zeros_like(dq_ref)
        dk_ref[...] = jnp.zeros_like(dk_ref)
        dv_ref[...] = jnp.zeros_like(dv_ref)


def tile_call(kernel, place, wide, stats, flops, order):
    width, count = wide[0].shape
    heads = width // HEAD_DIM
    wide_spec = pl.BlockSpec((HEAD_DIM, count), lambda h: (h, 0))
    stat_spec = pl.BlockSpec((1, 1, count), lambda h: (h, 0, 0))
    specs = {"w": wide_spec, "s": stat_spec}
    scalars = [] if place is None else [place]
    scalar_specs = [] if place is None else [pl.BlockSpec(memory_space=pltpu.SMEM)]
    wide_shape = jax.ShapeDtypeStruct((width, count), F32)
    stat_shape = jax.ShapeDtypeStruct((heads, 1, count), F32)
    ins, outs = order
    wide, stats = (list(wide), list(stats))
    args = [wide.pop(0) if kind == "w" else stats.pop(0) for kind in ins]
    return pl.pallas_call(
        kernel,
        grid=(heads,),
        in_specs=scalar_specs + [specs[kind] for kind in ins],
        out_specs=[specs[kind] for kind in outs],
        out_shape=[wide_shape if kind == "w" else stat_shape for kind in outs],
        compiler_params=pltpu.CompilerParams(vmem_limit_bytes=32 * 1024 * 1024),
        cost_estimate=pl.CostEstimate(
            flops=flops * 2 * width * count * count,
            bytes_accessed=6 * width * count * 4,
            transcendentals=heads * count * count,
        ),
    )(*scalars, *args)


def local(
    inputs,
    qkv_weight,
    qv_bias,
    out_weight,
    out_bias,
    up_weight,
    up_bias,
    down_weight,
    down_bias,
    first_gain,
    first_shift,
    second_gain,
    second_shift,
    grad_output,
):
    shape = inputs.shape
    width = shape[-1]
    rows = inputs.reshape(-1, width).astype(F32)
    count = rows.shape[0]
    ctx_size = lax.axis_size("ctx")
    dp_size = lax.axis_size("dp")
    dp_place = lax.axis_index("dp")
    place = lax.axis_index("ctx").astype(jnp.int32).reshape(1)

    kv_in = gather_shards(jnp.swapaxes(qkv_weight[:, 1:], 0, 1))
    kv_in = jnp.swapaxes(kv_in, 0, 1).reshape(2, width, -1)
    q_in = lax.all_gather(qkv_weight[:, 0], "dp", axis=0, tiled=True)
    small = (
        first_gain,
        first_shift,
        second_gain,
        second_shift,
        out_bias,
        down_bias,
        qv_bias,
        up_bias,
    )
    packed = lax.all_gather(jnp.concatenate([item.reshape(-1) for item in small]), "dp")
    packed = packed.astype(F32)
    parts = []
    start = 0
    for item in small:
        part = packed[:, start : start + item.size].reshape((dp_size,) + item.shape)
        start += item.size
        parts.append(jnp.moveaxis(part, 0, -2).reshape(item.shape[:-1] + (-1,)))
    gain_one, shift_one, gain_two, shift_two, bias_out, bias_down, bias_in, bias_up = parts
    attn_out = lax.all_gather(out_weight, "dp", axis=1, tiled=True)
    mlp_up = lax.all_gather(up_weight, "dp", axis=0, tiled=True)
    mlp_down = lax.all_gather(down_weight, "dp", axis=1, tiled=True)

    half_width = q_in.shape[1]
    heads = half_width // HEAD_DIM
    xhat_one, scale_one = norm_parts(rows)
    normed_low = (xhat_one * gain_one + shift_one).astype(BF16)
    bias_in = bias_in.reshape(2, half_width, 1)
    mixed = jnp.einsum("td,cdh->cht", normed_low, kv_in, preferred_element_type=F32)
    keys = mixed[0].astype(BF16)
    values = (mixed[1] + bias_in[1]).astype(BF16)

    blocks = [jnp.concatenate([keys, values], axis=0)]
    query = jnp.einsum("td,dh->ht", normed_low, q_in, preferred_element_type=F32)
    query = (query + bias_in[0]).astype(BF16)
    for distance in range(1, ctx_size):
        blocks.append(ahead(blocks[-1], "ctx", 1))
    peak, total, accum = tile_call(
        first_tile, None, (query, keys, values), (), 2, ("www", "ssw")
    )
    pairs = [(keys, values)]
    for distance in range(1, ctx_size):
        block = blocks[distance]
        pairs.append((block[:half_width], block[half_width:]))

        def step(*refs, distance=distance):
            next_tile(distance, *refs)

        peak, total, accum = tile_call(
            step,
            place,
            (query, *pairs[distance], accum),
            (peak, total),
            2,
            ("wwwssw", "ssw"),
        )
    attn_heads = accum.reshape(heads, HEAD_DIM, count) / total
    log_total = peak + jnp.log(total)
    attended_low = attn_heads.reshape(half_width, count).astype(BF16)

    branch = pair_sum(jnp.einsum("ht,hd->td", attended_low, attn_out, preferred_element_type=F32))
    resid = rows + branch + bias_out
    xhat_two, scale_two = norm_parts(resid)
    normed_two_low = (xhat_two * gain_two + shift_two).astype(BF16)
    hidden_pre = jnp.dot(normed_two_low, mlp_up, preferred_element_type=F32) + bias_up.reshape(-1)
    hidden_act, gelu_pull = jax.vjp(lambda pre: jax.nn.gelu(pre, approximate=True), hidden_pre)
    hidden_act = hidden_act.astype(BF16)

    grad_rows = grad_output.reshape(count, width)
    grad_float = grad_rows.astype(F32)
    grad_bias_down = jnp.sum(grad_float, axis=0)
    grad_act = jnp.einsum("td,fd->tf", grad_rows, mlp_down, preferred_element_type=F32)
    grad_pre = gelu_pull(grad_act)[0].astype(BF16)
    grad_normed_two = pair_sum(
        jnp.einsum("tf,df->td", grad_pre, mlp_up, preferred_element_type=F32)
    )

    grad_down = scatter_product(
        grad_rows,
        lambda part: jnp.einsum("tf,td->fd", hidden_act, part, preferred_element_type=F32),
    )
    grad_bias_up = jnp.sum(grad_pre, axis=0, dtype=F32)
    grad_up = scatter_product(
        normed_two_low,
        lambda part: jnp.einsum("td,tf->df", part, grad_pre, preferred_element_type=F32),
    )

    grad_gain_two = jnp.sum(grad_normed_two * xhat_two, axis=0)
    grad_shift_two = jnp.sum(grad_normed_two, axis=0)
    grad_resid = grad_float + norm_back(grad_normed_two, xhat_two, scale_two, gain_two)
    grad_branch = grad_resid.astype(BF16)
    grad_bias_out = jnp.sum(grad_branch, axis=0, dtype=F32)
    grad_attended = jnp.einsum(
        "td,hd->ht", grad_branch, attn_out, preferred_element_type=F32
    ).astype(BF16)
    grad_heads = grad_attended.astype(F32).reshape(heads, HEAD_DIM, count)
    delta = jnp.sum(grad_heads * attn_heads, axis=1, keepdims=True)
    grad_out = scatter_product(
        grad_branch,
        lambda part: jnp.einsum("ht,td->hd", attended_low, part, preferred_element_type=F32),
    )

    later_act, grad_attended = lax.optimization_barrier((hidden_act, grad_attended))
    mlp_part = jnp.dot(later_act, mlp_down, preferred_element_type=F32)
    mlp_part = pair_sum(mlp_part)

    grad_query = 0.0
    arrived = None
    for distance in range(ctx_size - 1, -1, -1):

        def back_step(*refs, distance=distance):
            back_tile(distance, *refs)

        part_query, part_keys, part_values = tile_call(
            back_step,
            place,
            (query, *pairs[distance], grad_attended),
            (log_total, delta),
            5,
            ("wwwwss", "www"),
        )
        grad_query = grad_query + part_query
        block = jnp.concatenate([part_keys, part_values], axis=0)
        if arrived is not None:
            block = block + arrived.astype(F32)
        block = block.astype(BF16)
        if distance > 0:
            arrived = ahead(block, "ctx", -1)
    mlp_part, block = lax.optimization_barrier((mlp_part, block))
    output = (resid + mlp_part + bias_down).astype(BF16).reshape(shape)
    grad_mixed = jnp.concatenate([grad_query.astype(BF16), block], axis=0)
    grad_mixed = grad_mixed.reshape(3, half_width, count)
    grad_bias_in = jnp.sum(grad_mixed[0::2], axis=2, dtype=F32)
    grad_normed_one = pair_sum(
        jnp.einsum("ht,dh->td", grad_mixed[0], q_in, preferred_element_type=F32)
        + jnp.einsum("cht,cdh->td", grad_mixed[1:], kv_in, preferred_element_type=F32)
    )
    grad_attn_in = scatter_product(
        normed_low,
        lambda part: jnp.einsum(
            "td,rt->dr", part, grad_mixed.reshape(-1, count), preferred_element_type=F32
        ),
    )
    grad_gain_one = jnp.sum(grad_normed_one * xhat_one, axis=0)
    grad_shift_one = jnp.sum(grad_normed_one, axis=0)
    grad_inputs = grad_resid + norm_back(grad_normed_one, xhat_one, scale_one, gain_one)
    grad_inputs = grad_inputs.astype(BF16).reshape(shape)

    grad_down, grad_up, grad_out = [line_total(item) for item in (grad_down, grad_up, grad_out)]
    grad_attn_in = ctx_total(grad_attn_in).reshape(-1, 3, half_width)

    grads_small = (
        grad_gain_one,
        grad_shift_one,
        grad_gain_two,
        grad_shift_two,
        grad_bias_out,
        grad_bias_down,
        grad_bias_in,
        grad_bias_up,
    )
    summed = small_total(jnp.concatenate([item.reshape(-1) for item in grads_small]))
    small_out = []
    start = 0
    for item in small:
        whole = summed[start : start + item.size * dp_size]
        start += item.size * dp_size
        whole = whole.reshape(item.shape[:-1] + (dp_size, item.shape[-1]))
        small_out.append(lax.dynamic_index_in_dim(whole, dp_place, whole.ndim - 2, False))
    (
        grad_gain_one,
        grad_shift_one,
        grad_gain_two,
        grad_shift_two,
        grad_bias_out,
        grad_bias_down,
        grad_bias_in,
        grad_bias_up,
    ) = small_out
    return (
        output,
        grad_inputs,
        grad_attn_in,
        grad_bias_in,
        grad_out,
        grad_bias_out,
        grad_up,
        grad_bias_up,
        grad_down,
        grad_bias_down,
        grad_gain_one,
        grad_shift_one,
        grad_gain_two,
        grad_shift_two,
    )


def solution(mesh):
    in_specs = (
        P("dp", "ctx", None),
        P("dp", None, "tensor"),
        P(None, "tensor", "dp"),
        P("tensor", "dp"),
        P("dp"),
        P("dp", "tensor"),
        P("tensor", "dp"),
        P("tensor", "dp"),
        P("dp"),
        P("dp"),
        P("dp"),
        P("dp"),
        P("dp"),
        P("dp", "ctx", None),
    )
    out_specs = (
        P("dp", "ctx", None),
        P("dp", "ctx", None),
        P("dp", None, "tensor"),
        P(None, "tensor", "dp"),
        P("tensor", "dp"),
        P("dp"),
        P("dp", "tensor"),
        P("tensor", "dp"),
        P("tensor", "dp"),
        P("dp"),
        P("dp"),
        P("dp"),
        P("dp"),
        P("dp"),
    )
    return jax.shard_map(local, mesh=mesh, in_specs=in_specs, out_specs=out_specs, check_vma=False)
```

```python
import jax
import jax.numpy as jnp
from jax import lax
from jax.experimental import pallas as pl
from jax.experimental.pallas import tpu as pltpu
from jax.sharding import PartitionSpec as P

HEAD_DIM = 64
F32 = jnp.float32
BF16 = jnp.bfloat16
ROWS_BY_ROWS = (((0,), (0,)), ((), ()))
LAST_BY_LAST = (((1,), (1,)), ((), ()))


def ahead(value, axis, steps):
    count = lax.axis_size(axis)
    first, last = (max(0, -steps), min(count, count - steps))
    return lax.ppermute(value, axis, [(source, source + steps) for source in range(first, last)])


def pair_sum(value):
    low = value.astype(BF16)
    if lax.axis_size("tensor") == 2:
        other = lax.ppermute(low, "tensor", [(0, 1), (1, 0)])
        return low.astype(F32) + other.astype(F32)
    return lax.psum(low, "tensor").astype(F32)


def flipped(value, axis, bit):
    count = lax.axis_size(axis)
    return lax.ppermute(value, axis, [(source, source ^ bit) for source in range(count)])


def gather_shards(shard):
    mine = lax.axis_index("dp")
    beside = flipped(shard, "dp", 1)
    across = flipped(shard, "dp", 2)
    corner = flipped(across, "dp", 1)
    whole = jnp.zeros((4,) + shard.shape, shard.dtype)
    for bit, item in enumerate((shard, beside, across, corner)):
        whole = lax.dynamic_update_index_in_dim(whole, item, mine ^ bit, 0)
    return whole


def shard_columns(rows, core, high):
    size = rows.shape[1] // 4
    return lax.dynamic_slice_in_dim(rows, (2 * high + core) * size, size, 1)


def scatter_product(rows, product):
    mine = lax.axis_index("dp")
    core, high = mine % 2, mine // 2
    sent = [product(shard_columns(rows, 1 - core, bit)).astype(BF16) for bit in (1 - high, high)]
    sent = [flipped(item, "dp", 1) for item in sent]
    kept = [product(shard_columns(rows, core, bit)) for bit in (1 - high, high)]
    away, home = [own + other.astype(F32) for own, other in zip(kept, sent)]
    return home + flipped(away.astype(BF16), "dp", 2).astype(F32)


def ctx_total(value):
    count = lax.axis_size("ctx")
    mine = lax.axis_index("ctx")
    chunks = value.astype(BF16).reshape((count, -1) + value.shape[1:])
    total = lax.dynamic_index_in_dim(chunks, mine, 0, False).astype(F32)
    for step in range(1, count):
        chunk = lax.dynamic_index_in_dim(chunks, (mine + step) % count, 0, False)
        pairs = [(source, (source + step) % count) for source in range(count)]
        total = total + lax.ppermute(chunk, "ctx", pairs).astype(F32)
    total = total.astype(BF16)
    whole = lax.dynamic_update_index_in_dim(jnp.zeros_like(chunks), total, mine, 0)
    for step in range(1, count):
        pairs = [(source, (source + step) % count) for source in range(count)]
        other = lax.ppermute(total, "ctx", pairs)
        whole = lax.dynamic_update_index_in_dim(whole, other, (mine + count - step) % count, 0)
    return whole.reshape(value.shape).astype(F32)


def small_total(value):
    for axis in ("dp", "ctx"):
        bit = 1
        while bit < lax.axis_size(axis):
            value = value + flipped(value, axis, bit)
            bit *= 2
    return value


def norm_parts(values):
    center = values - jnp.mean(values, axis=-1, keepdims=True)
    scale = lax.rsqrt(jnp.mean(center * center, axis=-1, keepdims=True) + 1e-05)
    return center * scale, scale


def norm_back(grad, xhat, scale, gain):
    scaled = grad * gain
    return scale * (
        scaled
        - jnp.mean(scaled, axis=-1, keepdims=True)
        - xhat * jnp.mean(scaled * xhat, axis=-1, keepdims=True)
    )


def causal(scores):
    key_pos = lax.broadcasted_iota(jnp.int32, scores.shape, 0)
    query_pos = lax.broadcasted_iota(jnp.int32, scores.shape, 1)
    return jnp.where(key_pos <= query_pos, scores, -1e30)


def scores_of(q_ref, k_ref):
    scaled = q_ref[...] * jnp.asarray(0.125, BF16)
    return lax.dot_general(k_ref[...], scaled, ROWS_BY_ROWS, preferred_element_type=F32)


def first_tile(q_ref, k_ref, v_ref, peak_ref, total_ref, accum_ref):
    scores = causal(scores_of(q_ref, k_ref))
    peak = jnp.max(scores, axis=0, keepdims=True)
    weights = jnp.exp(scores - peak)
    peak_ref[0] = peak
    total_ref[0] = jnp.sum(weights, axis=0, keepdims=True)
    accum_ref[...] = jnp.dot(v_ref[...], weights.astype(BF16), preferred_element_type=F32)


def next_tile(distance, place_ref, q_ref, k_ref, v_ref, p_ref, t_ref, a_ref, peak_ref, total_ref, accum_ref):
    valid = place_ref[0] >= distance

    @pl.when(valid)
    def run():
        scores = scores_of(q_ref, k_ref)
        old = p_ref[0]
        peak = jnp.maximum(old, jnp.max(scores, axis=0, keepdims=True))
        weights = jnp.exp(scores - peak)
        fade = jnp.exp(old - peak)
        peak_ref[0] = peak
        total_ref[0] = t_ref[0] * fade + jnp.sum(weights, axis=0, keepdims=True)
        accum_ref[...] = a_ref[...] * fade + jnp.dot(
            v_ref[...], weights.astype(BF16), preferred_element_type=F32
        )

    @pl.when(jnp.logical_not(valid))
    def keep():
        peak_ref[...] = p_ref[...]
        total_ref[...] = t_ref[...]
        accum_ref[...] = a_ref[...]


def back_tile(distance, place_ref, q_ref, k_ref, v_ref, g_ref, lse_ref, delta_ref, dq_ref, dk_ref, dv_ref):
    valid = place_ref[0] >= distance

    @pl.when(valid)
    def run():
        scores = scores_of(q_ref, k_ref)
        if distance == 0:
            scores = causal(scores)
        probs = jnp.exp(scores - lse_ref[0])
        grad_probs = lax.dot_general(
            v_ref[...], g_ref[...], ROWS_BY_ROWS, preferred_element_type=F32
        )
        grad_scores = (probs * (grad_probs - delta_ref[0])).astype(BF16)
        dv_ref[...] = lax.dot_general(
            g_ref[...], probs.astype(BF16), LAST_BY_LAST, preferred_element_type=F32
        )
        dk_ref[...] = 0.125 * lax.dot_general(
            q_ref[...], grad_scores, LAST_BY_LAST, preferred_element_type=F32
        )
        dq_ref[...] = 0.125 * jnp.dot(k_ref[...], grad_scores, preferred_element_type=F32)

    @pl.when(jnp.logical_not(valid))
    def clear():
        dq_ref[...] = jnp.zeros_like(dq_ref)
        dk_ref[...] = jnp.zeros_like(dk_ref)
        dv_ref[...] = jnp.zeros_like(dv_ref)


def tile_call(kernel, place, wide, stats, flops, order):
    width, count = wide[0].shape
    heads = width // HEAD_DIM
    wide_spec = pl.BlockSpec((HEAD_DIM, count), lambda h: (h, 0))
    stat_spec = pl.BlockSpec((1, 1, count), lambda h: (h, 0, 0))
    specs = {"w": wide_spec, "s": stat_spec}
    scalars = [] if place is None else [place]
    scalar_specs = [] if place is None else [pl.BlockSpec(memory_space=pltpu.SMEM)]
    wide_shape = jax.ShapeDtypeStruct((width, count), F32)
    stat_shape = jax.ShapeDtypeStruct((heads, 1, count), F32)
    ins, outs = order
    wide, stats = (list(wide), list(stats))
    args = [wide.pop(0) if kind == "w" else stats.pop(0) for kind in ins]
    return pl.pallas_call(
        kernel,
        grid=(heads,),
        in_specs=scalar_specs + [specs[kind] for kind in ins],
        out_specs=[specs[kind] for kind in outs],
        out_shape=[wide_shape if kind == "w" else stat_shape for kind in outs],
        compiler_params=pltpu.CompilerParams(vmem_limit_bytes=32 * 1024 * 1024),
        cost_estimate=pl.CostEstimate(
            flops=flops * 2 * width * count * count,
            bytes_accessed=6 * width * count * 4,
            transcendentals=heads * count * count,
        ),
    )(*scalars, *args)


def local(
    inputs,
    qkv_weight,
    qv_bias,
    out_weight,
    out_bias,
    up_weight,
    up_bias,
    down_weight,
    down_bias,
    first_gain,
    first_shift,
    second_gain,
    second_shift,
    grad_output,
):
    shape = inputs.shape
    width = shape[-1]
    rows = inputs.reshape(-1, width).astype(F32)
    count = rows.shape[0]
    ctx_size = lax.axis_size("ctx")
    dp_size = lax.axis_size("dp")
    dp_place = lax.axis_index("dp")
    place = lax.axis_index("ctx").astype(jnp.int32).reshape(1)

    kv_in = gather_shards(jnp.swapaxes(qkv_weight[:, 1:], 0, 1))
    kv_in = jnp.swapaxes(kv_in, 0, 1).reshape(2, width, -1)
    q_in = lax.all_gather(qkv_weight[:, 0], "dp", axis=0, tiled=True)
    small = (
        first_gain,
        first_shift,
        second_gain,
        second_shift,
        out_bias,
        down_bias,
        qv_bias,
        up_bias,
    )
    packed = lax.all_gather(jnp.concatenate([item.reshape(-1) for item in small]), "dp")
    packed = packed.astype(F32)
    parts = []
    start = 0
    for item in small:
        part = packed[:, start : start + item.size].reshape((dp_size,) + item.shape)
        start += item.size
        parts.append(jnp.moveaxis(part, 0, -2).reshape(item.shape[:-1] + (-1,)))
    gain_one, shift_one, gain_two, shift_two, bias_out, bias_down, bias_in, bias_up = parts
    attn_out = lax.all_gather(out_weight, "dp", axis=1, tiled=True)
    mlp_up = lax.all_gather(up_weight, "dp", axis=0, tiled=True)
    mlp_down = lax.all_gather(down_weight, "dp", axis=1, tiled=True)

    half_width = q_in.shape[1]
    heads = half_width // HEAD_DIM
    xhat_one, scale_one = norm_parts(rows)
    normed_low = (xhat_one * gain_one + shift_one).astype(BF16)
    bias_in = bias_in.reshape(2, half_width, 1)
    mixed = jnp.einsum("td,cdh->cht", normed_low, kv_in, preferred_element_type=F32)
    keys = mixed[0].astype(BF16)
    values = (mixed[1] + bias_in[1]).astype(BF16)

    blocks = [jnp.concatenate([keys, values], axis=0)]
    query = jnp.einsum("td,dh->ht", normed_low, q_in, preferred_element_type=F32)
    query = (query + bias_in[0]).astype(BF16)
    for distance in range(1, ctx_size):
        blocks.append(ahead(blocks[-1], "ctx", 1))
    peak, total, accum = tile_call(
        first_tile, None, (query, keys, values), (), 2, ("www", "ssw")
    )
    pairs = [(keys, values)]
    for distance in range(1, ctx_size):
        block = blocks[distance]
        pairs.append((block[:half_width], block[half_width:]))

        def step(*refs, distance=distance):
            next_tile(distance, *refs)

        peak, total, accum = tile_call(
            step,
            place,
            (query, *pairs[distance], accum),
            (peak, total),
            2,
            ("wwwssw", "ssw"),
        )
    attn_heads = accum.reshape(heads, HEAD_DIM, count) / total
    log_total = peak + jnp.log(total)
    attended_low = attn_heads.reshape(half_width, count).astype(BF16)

    branch = pair_sum(jnp.einsum("ht,hd->td", attended_low, attn_out, preferred_element_type=F32))
    resid = rows + branch + bias_out
    xhat_two, scale_two = norm_parts(resid)
    normed_two_low = (xhat_two * gain_two + shift_two).astype(BF16)
    hidden_pre = jnp.dot(normed_two_low, mlp_up, preferred_element_type=F32) + bias_up.reshape(-1)
    hidden_act, gelu_pull = jax.vjp(lambda pre: jax.nn.gelu(pre, approximate=True), hidden_pre)
    hidden_act = hidden_act.astype(BF16)

    grad_rows = grad_output.reshape(count, width)
    grad_float = grad_rows.astype(F32)
    grad_bias_down = jnp.sum(grad_float, axis=0)
    grad_act = jnp.einsum("td,fd->tf", grad_rows, mlp_down, preferred_element_type=F32)
    grad_pre = gelu_pull(grad_act)[0].astype(BF16)
    grad_normed_two = pair_sum(
        jnp.einsum("tf,df->td", grad_pre, mlp_up, preferred_element_type=F32)
    )
    later_act, grad_normed_two = lax.optimization_barrier((hidden_act, grad_normed_two))
    mlp_part = pair_sum(jnp.dot(later_act, mlp_down, preferred_element_type=F32))

    grad_down = scatter_product(
        grad_rows,
        lambda part: jnp.einsum("tf,td->fd", hidden_act, part, preferred_element_type=F32),
    )
    grad_bias_up = jnp.sum(grad_pre, axis=0, dtype=F32)
    grad_up = scatter_product(
        normed_two_low,
        lambda part: jnp.einsum("td,tf->df", part, grad_pre, preferred_element_type=F32),
    )

    grad_gain_two = jnp.sum(grad_normed_two * xhat_two, axis=0)
    grad_shift_two = jnp.sum(grad_normed_two, axis=0)
    grad_resid = grad_float + norm_back(grad_normed_two, xhat_two, scale_two, gain_two)
    grad_branch = grad_resid.astype(BF16)
    grad_bias_out = jnp.sum(grad_branch, axis=0, dtype=F32)
    grad_attended = jnp.einsum(
        "td,hd->ht", grad_branch, attn_out, preferred_element_type=F32
    ).astype(BF16)
    grad_heads = grad_attended.astype(F32).reshape(heads, HEAD_DIM, count)
    delta = jnp.sum(grad_heads * attn_heads, axis=1, keepdims=True)
    grad_out = scatter_product(
        grad_branch,
        lambda part: jnp.einsum("ht,td->hd", attended_low, part, preferred_element_type=F32),
    )

    grad_query = 0.0
    arrived = None
    for distance in range(ctx_size - 1, -1, -1):

        def back_step(*refs, distance=distance):
            back_tile(distance, *refs)

        part_query, part_keys, part_values = tile_call(
            back_step,
            place,
            (query, *pairs[distance], grad_attended),
            (log_total, delta),
            5,
            ("wwwwss", "www"),
        )
        grad_query = grad_query + part_query
        block = jnp.concatenate([part_keys, part_values], axis=0)
        if arrived is not None:
            block = block + arrived.astype(F32)
        block = block.astype(BF16)
        if distance > 0:
            arrived = ahead(block, "ctx", -1)
    mlp_part, block = lax.optimization_barrier((mlp_part, block))
    output = (resid + mlp_part + bias_down).astype(BF16).reshape(shape)
    grad_mixed = jnp.concatenate([grad_query.astype(BF16), block], axis=0)
    grad_mixed = grad_mixed.reshape(3, half_width, count)
    grad_bias_in = jnp.sum(grad_mixed[0::2], axis=2, dtype=F32)
    grad_normed_one = pair_sum(
        jnp.einsum("ht,dh->td", grad_mixed[0], q_in, preferred_element_type=F32)
        + jnp.einsum("cht,cdh->td", grad_mixed[1:], kv_in, preferred_element_type=F32)
    )
    grad_attn_in = scatter_product(
        normed_low,
        lambda part: jnp.einsum(
            "td,rt->dr", part, grad_mixed.reshape(-1, count), preferred_element_type=F32
        ),
    )
    grad_gain_one = jnp.sum(grad_normed_one * xhat_one, axis=0)
    grad_shift_one = jnp.sum(grad_normed_one, axis=0)
    grad_inputs = grad_resid + norm_back(grad_normed_one, xhat_one, scale_one, gain_one)
    grad_inputs = grad_inputs.astype(BF16).reshape(shape)

    sums = [lax.psum(item.astype(BF16), "ctx") for item in (grad_up, grad_down, grad_out)]
    grad_attn_in = ctx_total(grad_attn_in)
    sums, grad_attn_in = lax.optimization_barrier((sums, grad_attn_in))
    grad_up, grad_down, grad_out = [item.astype(F32) for item in sums]
    grad_attn_in = grad_attn_in.reshape(-1, 3, half_width)

    grads_small = (
        grad_gain_one,
        grad_shift_one,
        grad_gain_two,
        grad_shift_two,
        grad_bias_out,
        grad_bias_down,
        grad_bias_in,
        grad_bias_up,
    )
    summed = small_total(jnp.concatenate([item.reshape(-1) for item in grads_small]))
    small_out = []
    start = 0
    for item in small:
        whole = summed[start : start + item.size * dp_size]
        start += item.size * dp_size
        whole = whole.reshape(item.shape[:-1] + (dp_size, item.shape[-1]))
        small_out.append(lax.dynamic_index_in_dim(whole, dp_place, whole.ndim - 2, False))
    (
        grad_gain_one,
        grad_shift_one,
        grad_gain_two,
        grad_shift_two,
        grad_bias_out,
        grad_bias_down,
        grad_bias_in,
        grad_bias_up,
    ) = small_out
    return (
        output,
        grad_inputs,
        grad_attn_in,
        grad_bias_in,
        grad_out,
        grad_bias_out,
        grad_up,
        grad_bias_up,
        grad_down,
        grad_bias_down,
        grad_gain_one,
        grad_shift_one,
        grad_gain_two,
        grad_shift_two,
    )


def solution(mesh):
    in_specs = (
        P("dp", "ctx", None),
        P("dp", None, "tensor"),
        P(None, "tensor", "dp"),
        P("tensor", "dp"),
        P("dp"),
        P("dp", "tensor"),
        P("tensor", "dp"),
        P("tensor", "dp"),
        P("dp"),
        P("dp"),
        P("dp"),
        P("dp"),
        P("dp"),
        P("dp", "ctx", None),
    )
    out_specs = (
        P("dp", "ctx", None),
        P("dp", "ctx", None),
        P("dp", None, "tensor"),
        P(None, "tensor", "dp"),
        P("tensor", "dp"),
        P("dp"),
        P("dp", "tensor"),
        P("tensor", "dp"),
        P("tensor", "dp"),
        P("dp"),
        P("dp"),
        P("dp"),
        P("dp"),
        P("dp"),
    )
    return jax.shard_map(local, mesh=mesh, in_specs=in_specs, out_specs=out_specs, check_vma=False)
```
